32 devices in a mesh: wide: 4 (over y, core), narrow: 8 (over z, x).
Axes of the slice: x: 2, y: 2, z: 4, core: 2. Of those that a mesh axis runs over, the one named last changes fastest.
Arguments:
- queries: bfloat16 [8192, 128], P(('wide', 'narrow')), may hold values from -6 to 6
- index_rows: bfloat16 [262144, 128], P(('wide', 'narrow')), may hold values from -6 to 6
- lse_shift: float32 [8192], P('wide'), may hold values from 0 to 2.5
- loss_weight: float32 [8192], P('wide'), may hold values from 4 to 32
- positives: int32 [8192], P('wide'), may hold values from 0 to 16383
- tile_negs: int32 [64, 64], P('wide'), may hold values from 0 to 127
- fetch_owner: int32 [512, 1], P(('wide', 'narrow')), may hold values from 0 to 31; in each aligned block of 16 rows (0 to 15, 16 to 31, ...) at most 2 rows name the same one
- fetch_local: int32 [512], P(('wide', 'narrow')), may hold values from 0 to 63
Outputs:
- query_grad: float32 [8192, 128], P(('wide', 'narrow'))
- index_grad: float32 [262144, 128], P(('wide', 'narrow'))
The draws below stay inside these ranges and needn't reach their ends.
Inputs may be any that keep to these rules, and one draw needn't show every extreme that they name: `fetch_owner`: among the 16 fetches of one device no owner is named more than 2 times, a bound that some block reaches.
All inputs are finite; a program needn't handle non-finite values.
Results may differ from the reference program's by a relative error of at most 0.0043.
Values may be sent and summed in bfloat16 or wider, within the bound.
A program may use at most 128 MiB of HBM per device.

```python
import math
import jax
import jax.numpy as jnp
import numpy as np
from jax import lax

D = 128
BLOCK = 128
QTILE = 128
CAP = 2
NB_DEV = 64
FETCH = 16
Q_GRP = 2048
QUERIES = 8192
SLOTS_GRP = 128
KT = 64
TILES = 64
INDEX_ROWS = 262144
N_WIDE = 4
N_NARROW = 8
DEVICES = 32


def with_ends(result, own_key, least, largest):
    longest = result.shape.index(max(result.shape))
    spots = []
    for shift in (0, 1):
        where = [jax.random.randint(jax.random.fold_in(own_key, axis), (), 0, length) for axis, length in enumerate(result.shape)]
        where[longest] = (where[longest] + shift) % result.shape[longest]
        spots.append(tuple(where))
    return result.at[spots[0]].set(least).at[spots[1]].set(largest)


def levels(rng, dims, shards, least, top_value):
    gain = 1.0
    for dim, blocks in shards:
        steps = jax.random.uniform(jax.random.fold_in(jax.random.fold_in(rng, 6), dim), (blocks,), jnp.float32, least / len(shards), top_value / len(shards))
        gain = gain * jnp.repeat(jnp.exp(steps), dims[dim] // blocks).reshape((-1,) + (1,) * (len(dims) - 1 - dim))
    return gain


def assign_block(key, own, number, rows, count, top, limit, lean):
    sequence = jax.random.permutation(key, count)
    packed, usual = shares(count, rows * top, limit, lean, True), shares(count, rows * top, limit, lean, False)
    places = jnp.arange(count)

    def named(lengths, turn):
        used = int((lengths > 0).sum())
        fixed = max(1, used // 4)
        moved = fixed + (places - fixed + turn * (used - fixed)) % max(1, count - fixed)
        return jnp.zeros((count,), jnp.int32).at[sequence[jnp.where(places < fixed, places, moved)]].set(jnp.asarray(lengths, jnp.int32))

    lengths = jnp.where(number % 4 == 0, named(packed, number // 4), named(usual, number - number // 4 - 1))
    mixed = jax.random.permutation(jax.random.fold_in(own, 3), count)
    donor, sink = mixed[0:count // 2 * 2:2], mixed[1:count // 2 * 2:2]
    room = jnp.minimum(lengths[donor] - 1, limit - lengths[sink]) // 2
    room = jnp.where((donor == sequence[0]) | (sink == sequence[0]) | (lengths[sink] == 0), 0, jnp.maximum(room, 0))
    moved = jax.random.randint(jax.random.fold_in(own, 4), (count // 2,), 0, 1 << 20) % (room + 1)
    lengths = lengths.at[donor].add(-moved).at[sink].add(moved)
    labels = jnp.searchsorted(jnp.cumsum(lengths), jnp.arange(rows * top), side="right").astype(jnp.int32)
    grid = labels.reshape(top, rows).T
    grid = grid[jax.random.permutation(jax.random.fold_in(own, 1), rows)]
    turn = jax.random.randint(jax.random.fold_in(own, 2), (rows, 1), 0, top)
    return jnp.take_along_axis(grid, (jnp.arange(top)[None, :] + turn) % top, axis=1)


def shares(count, total, limit, skew, full):
    loads = [(1 << 20) // math.isqrt(rank ** skew) + 1 for rank in range(1, count + 1)]
    largest = limit if full else min(limit, max(-(-total // count), total * loads[0] // sum(loads)))
    least = 1 if total - largest >= count - 1 else 0
    counts, surplus = [largest] + [least] * (count - 1), total - largest - least * (count - 1)
    while surplus > 0:
        free = [i for i in range(1, count) if counts[i] < largest] or [i for i in range(1, count) if counts[i] < limit]
        whole, remaining = sum([loads[i] for i in free]), surplus
        for i in free:
            more = min(limit - counts[i], max(1, remaining * loads[i] // whole), surplus)
            counts[i] = counts[i] + more
            surplus = surplus - more
    return np.array(counts)


def bell_draw(rng, extent, scale, reach, shards=(), kind=jnp.bfloat16):
    factor_of = levels(rng, extent, shards, -0.22, 0.18) if shards else 1.0
    entries = jax.random.normal(rng, extent, jnp.float32) * scale * factor_of
    return jnp.minimum(jnp.maximum(entries, -reach), reach).astype(kind)


def setup_inputs(seed: int = 0) -> dict:
    seeds = jax.random.split(jax.random.key(seed), 9)
    queries = bell_draw(seeds[0], (QUERIES, D), 1.0, 6.0, ((0, 32),))
    index_rows = bell_draw(seeds[1], (INDEX_ROWS, D), 1.0, 6.0, ((0, 32),))
    lse_shift = jnp.clip(2.5 * jax.random.uniform(seeds[2], (QUERIES,), jnp.float32) ** levels(seeds[2], (QUERIES,), ((0, 4),), -0.2, 0.2), 0.0, 2.5)
    loss_weight = jnp.clip(jnp.exp(math.log(32.0) - 2.0794415 * jax.random.uniform(seeds[3], (QUERIES,), jnp.float32) ** levels(seeds[3], (QUERIES,), ((0, 4),), -0.2, 0.2)), 4.0, 32.0)
    positives = with_ends(jax.random.randint(seeds[4], (QUERIES,), 0, SLOTS_GRP * BLOCK), jax.random.fold_in(seeds[4], 1), 0, (SLOTS_GRP * BLOCK) - 1).astype(jnp.int32)
    tile_negs = with_ends(jax.random.randint(seeds[5], (TILES, KT), 0, SLOTS_GRP), jax.random.fold_in(seeds[5], 1), 0, SLOTS_GRP - 1).astype(jnp.int32)
    fetch_owner_keys = jax.random.split(jax.random.fold_in(seeds[6], 1), (DEVICES * FETCH) // FETCH)
    fetch_owner_turns = jax.random.permutation(jax.random.fold_in(seeds[6], 3), (DEVICES * FETCH) // FETCH)
    fetch_owner = jax.vmap(lambda own, number: assign_block(jax.random.fold_in(seeds[6], 2), own, number, FETCH, DEVICES, 1, CAP, 2))(fetch_owner_keys, fetch_owner_turns).reshape((DEVICES * FETCH, 1))
    fetch_local = with_ends(jax.random.randint(seeds[7], (DEVICES * FETCH,), 0, NB_DEV), jax.random.fold_in(seeds[7], 1), 0, NB_DEV - 1).astype(jnp.int32)
    return dict(queries=queries, index_rows=index_rows, lse_shift=lse_shift, loss_weight=loss_weight, positives=positives, tile_negs=tile_negs, fetch_owner=fetch_owner, fetch_local=fetch_local)


def device_terms(group_queries, lse_full, loss_rows, pos_rows, negs_rows, fetched, narrow_pos):
    score_scale = 2.0 / math.sqrt(D)
    column_count = FETCH * BLOCK
    scores = jnp.dot(group_queries, fetched.T, preferred_element_type=jnp.float32) * score_scale
    slot_ids = narrow_pos * FETCH + jnp.arange(FETCH, dtype=jnp.int32)
    tile_hit = jnp.any(negs_rows[:, :, None] == slot_ids[None, None, :], axis=1)
    query_hit = jnp.repeat(tile_hit, QTILE, axis=0)
    pos_hit = (pos_rows // BLOCK)[:, None] == slot_ids[None, :]
    weight = jnp.logical_or(query_hit, pos_hit).astype(jnp.float32)
    weight = jnp.repeat(weight, BLOCK, axis=1)
    column_ids = narrow_pos * column_count + jnp.arange(column_count, dtype=jnp.int32)
    target = (pos_rows[:, None] == column_ids[None, :]).astype(jnp.float32)
    softmax_terms = jnp.exp(scores - lse_full[:, None])
    logit_grad = (loss_rows[:, None] * (weight * softmax_terms - target)).astype(jnp.bfloat16)
    query_part = jnp.dot(logit_grad, fetched, preferred_element_type=jnp.float32) * score_scale
    block_part = (jnp.dot(logit_grad.T, group_queries, preferred_element_type=jnp.float32) * score_scale).astype(jnp.bfloat16)
    return (query_part, block_part)

def reference(queries, index_rows, lse_shift, loss_weight, positives, tile_negs, fetch_owner, fetch_local):
    device_total = N_WIDE * N_NARROW
    index_blocks = index_rows.reshape(device_total * NB_DEV, BLOCK, D)
    lse_all = lse_shift + math.log(SLOTS_GRP * BLOCK)
    tile_count = Q_GRP // QTILE

    def one_device(totals, device):
        query_grad, index_grad = totals
        group_idx = device // N_NARROW
        narrow_pos = device % N_NARROW
        first = group_idx * Q_GRP
        group_queries = lax.dynamic_slice_in_dim(queries, first, Q_GRP, 0)
        lse_rows = lax.dynamic_slice_in_dim(lse_all, first, Q_GRP, 0)
        loss_rows = lax.dynamic_slice_in_dim(loss_weight, first, Q_GRP, 0)
        pos_rows = lax.dynamic_slice_in_dim(positives, first, Q_GRP, 0)
        negs_rows = lax.dynamic_slice_in_dim(tile_negs, group_idx * tile_count, tile_count, 0)
        owners = lax.dynamic_slice_in_dim(fetch_owner[:, 0], device * FETCH, FETCH, 0)
        local_ids = lax.dynamic_slice_in_dim(fetch_local, device * FETCH, FETCH, 0)
        block_ids = (owners * NB_DEV + local_ids).astype(jnp.int32)
        fetched = jnp.take(index_blocks, block_ids, axis=0).reshape(FETCH * BLOCK, D)
        query_part, block_part = device_terms(group_queries, lse_rows, loss_rows, pos_rows, negs_rows, fetched, narrow_pos)
        current = lax.dynamic_slice_in_dim(query_grad, first, Q_GRP, 0)
        query_grad = lax.dynamic_update_slice_in_dim(query_grad, current + query_part, first, 0)
        index_grad = index_grad.at[block_ids].add(block_part.reshape(FETCH, BLOCK, D).astype(jnp.float32))
        return ((query_grad, index_grad), None)
    zeros_init = (jnp.zeros((QUERIES, D), jnp.float32), jnp.zeros((device_total * NB_DEV, BLOCK, D), jnp.float32))
    (query_grad, index_grad), unused = lax.scan(one_device, zeros_init, jnp.arange(device_total, dtype=jnp.int32))
    return (query_grad, index_grad.reshape(INDEX_ROWS, D))
```

```python
import functools
import math

import jax
import jax.numpy as jnp
from jax import lax
from jax.experimental import pallas as pl
from jax.experimental.pallas import tpu as pltpu
from jax.sharding import PartitionSpec as P

BLOCK = 128
QTILE = 128
CAP = 2
LANES = 128
CORES = 2
MESH = pl.DeviceIdType.MESH
VMEM_LIMIT = 56 * 1024 * 1024
FAR_BELOW = -1e30


def place_counts(wide_count, narrow_count):
    x_count = 1 << (int(math.log2(narrow_count)) // 2)
    return wide_count // CORES, narrow_count // x_count, x_count


def coordinates(x_count):
    wide, narrow = lax.axis_index("wide"), lax.axis_index("narrow")
    return wide // CORES, wide % CORES, narrow // x_count, narrow % x_count


def greet(peers):
    barrier = pltpu.get_barrier_semaphore()
    for peer in peers:
        pl.semaphore_signal(barrier, inc=1, device_id=peer, device_id_type=MESH)
    pl.semaphore_wait(barrier, len(peers))


def gather_kernel(
    y_count, z_count, x_count, query_ref, aux_ref, query_all, aux_all, own_sem, *sems
):
    y, core, z, x = coordinates(x_count)
    narrow_count = z_count * x_count

    def device(dy, other, dz, dx):
        wide = lax.rem(y + dy, y_count) * CORES + (1 - core if other else core)
        return wide, lax.rem(z + dz, z_count) * x_count + lax.rem(x + dx, x_count)

    def number(place):
        return place[0] * narrow_count + place[1]

    plane = [(dy, dx) for dy in range(y_count) for dx in range(x_count)][1:]
    z_peers = [device(0, False, dz, 0) for dz in range(1, z_count)]
    plane_peers = [device(dy, False, 0, dx) for dy, dx in plane]
    buddy = device(0, True, 0, 0)
    greet(z_peers + plane_peers + [buddy])
    me = number(device(0, False, 0, 0))
    pairs = (
        (query_ref, query_all, sems[0], sems[1]),
        (aux_ref, aux_all, sems[2], sems[3]),
    )
    sent = []

    def send(chunk, peer, own):
        for source, whole, send_sem, recv_sem in pairs:
            copy = pltpu.make_async_remote_copy(
                src_ref=source if own else whole.at[chunk],
                dst_ref=whole.at[chunk],
                send_sem=send_sem.at[len(sent) // 2],
                recv_sem=recv_sem.at[chunk],
                device_id=peer,
                device_id_type=MESH,
            )
            copy.start()
            sent.append(copy)

    def arrive(chunk):
        for source, whole, send_sem, recv_sem in pairs:
            pltpu.make_async_remote_copy(
                src_ref=source,
                dst_ref=whole.at[chunk],
                send_sem=send_sem.at[0],
                recv_sem=recv_sem.at[chunk],
                device_id=buddy,
                device_id_type=MESH,
            ).wait_recv()

    local = [
        pltpu.make_async_copy(source, whole.at[me], own_sem.at[i])
        for i, (source, whole, _, _) in enumerate(pairs)
    ]
    for copy in local:
        copy.start()
    for peer in z_peers + plane_peers + [buddy]:
        send(me, peer, True)
    for dz in range(1, z_count):
        chunk = number(device(0, False, dz, 0))
        arrive(chunk)
        for peer in plane_peers + [buddy]:
            send(chunk, peer, False)
    for dz in range(z_count):
        for dy, dx in plane:
            chunk = number(device(dy, False, dz, dx))
            arrive(chunk)
            send(chunk, buddy, False)
    for dz in range(z_count):
        for dy, dx in [(0, 0)] + plane:
            arrive(number(device(dy, True, dz, dx)))
    for copy in sent:
        copy.wait_send()
    for copy in local:
        copy.wait()


def gather_all(queries, aux, counts):
    y_count, z_count, x_count = counts
    devices = y_count * CORES * z_count * x_count
    in_plane = y_count * x_count
    sends = (z_count - 1) + (in_plane - 1) * z_count + in_plane * z_count
    return pl.pallas_call(
        functools.partial(gather_kernel, *counts),
        out_shape=(
            jax.ShapeDtypeStruct((devices, *queries.shape), queries.dtype),
            jax.ShapeDtypeStruct((devices, *aux.shape), aux.dtype),
        ),
        in_specs=[pl.BlockSpec(memory_space=pltpu.VMEM)] * 2,
        out_specs=[pl.BlockSpec(memory_space=pltpu.VMEM)] * 2,
        scratch_shapes=[
            pltpu.SemaphoreType.DMA((2,)),
            pltpu.SemaphoreType.DMA((sends,)),
            pltpu.SemaphoreType.DMA((devices,)),
            pltpu.SemaphoreType.DMA((sends,)),
            pltpu.SemaphoreType.DMA((devices,)),
        ],
        compiler_params=pltpu.CompilerParams(
            collective_id=0, has_side_effects=True, vmem_limit_bytes=VMEM_LIMIT
        ),
    )(queries, aux)


def work_kernel(
    score_scale,
    me_ref,
    owner_ref,
    local_ref,
    index_ref,
    query_ref,
    bias_ref,
    loss_ref,
    pos_ref,
    negs_ref,
    dq_ref,
    index_grad_ref,
    names,
    bias_now,
    rel_now,
    block_sum,
):
    fetch_total = owner_ref.shape[0]
    tile_total = bias_ref.shape[0]
    groups = lax.axis_size("wide")
    group_tiles = tile_total // groups
    group_slots = fetch_total // groups
    chunk_tiles = min(4, group_tiles)
    chunk = chunk_tiles * QTILE
    me = me_ref[0]
    log2_scale = score_scale * math.log2(math.e)

    def list_one(i, count):
        names[count] = i
        return count + (owner_ref[i] == me).astype(jnp.int32)

    count = lax.fori_loop(0, fetch_total, list_one, jnp.int32(0), unroll=8)
    dq_ref[...] = jnp.zeros_like(dq_ref)
    index_grad_ref[...] = jnp.zeros_like(index_grad_ref)
    row_ids = lax.broadcasted_iota(jnp.int32, (BLOCK, QTILE), 0)

    @pl.loop(0, count)
    def _(i):
        fetch = names[i]
        group = fetch // group_slots
        slot = fetch % group_slots
        rows = pl.ds(pl.multiple_of(local_ref[fetch] * BLOCK, BLOCK), BLOCK)
        block = index_ref[rows, :]
        block_t = block.astype(jnp.float32).T.astype(jnp.bfloat16)
        tiles = pl.ds(pl.multiple_of(group * group_tiles, 8), group_tiles)
        hit = jnp.any(negs_ref[tiles, :] == slot, axis=1, keepdims=True)
        rel = pos_ref[tiles, :] - slot * BLOCK
        inside = jnp.logical_and(rel >= 0, rel < BLOCK)
        bias_now[...] = jnp.where(jnp.logical_or(hit, inside), bias_ref[tiles, :], FAR_BELOW)
        rel_now[...] = rel
        block_sum[...] = jnp.zeros_like(block_sum)
        for turn in range(group_tiles // chunk_tiles):
            first = group * group_tiles + turn * chunk_tiles
            query = query_ref[pl.ds(pl.multiple_of(first * QTILE, chunk), chunk), :]
            scores = lax.dot_general(
                block, query, (((1,), (1,)), ((), ())), preferred_element_type=jnp.float32
            )
            parts = []
            for t in range(chunk_tiles):
                at = turn * chunk_tiles + t
                grown = jnp.exp2(
                    scores[:, t * QTILE : (t + 1) * QTILE] * log2_scale + bias_now[at : at + 1, :]
                )
                less = grown - loss_ref[pl.ds(first + t, 1), :]
                grad = jnp.where(row_ids == rel_now[at : at + 1, :], less, grown)
                parts.append(grad.astype(jnp.bfloat16))
            logit_grad = jnp.concatenate(parts, axis=1)
            block_sum[...] += jnp.dot(logit_grad, query, preferred_element_type=jnp.float32)
            part = jnp.dot(block_t, logit_grad, preferred_element_type=jnp.float32)
            for t in range(chunk_tiles):
                dq_ref[first + t] += part[:, t * QTILE : (t + 1) * QTILE]
        term = (block_sum[...] * score_scale).astype(jnp.bfloat16).astype(jnp.float32)
        index_grad_ref[rows, :] += term


def work(me, owner, local, index_rows, query_all, bias, loss, pos, negs, score_scale):
    feat_width = index_rows.shape[1]
    tile_total = bias.shape[0]
    group_tiles = tile_total // lax.axis_size("wide")
    smem, vmem = (pl.BlockSpec(memory_space=m) for m in (pltpu.SMEM, pltpu.VMEM))
    return pl.pallas_call(
        functools.partial(work_kernel, score_scale),
        out_shape=(
            jax.ShapeDtypeStruct((tile_total, feat_width, QTILE), jnp.float32),
            jax.ShapeDtypeStruct(index_rows.shape, jnp.float32),
        ),
        in_specs=[smem] * 3 + [vmem] * 6,
        out_specs=[vmem] * 2,
        scratch_shapes=[
            pltpu.SMEM((owner.shape[0] + 1,), jnp.int32),
            pltpu.VMEM((group_tiles, QTILE), jnp.float32),
            pltpu.VMEM((group_tiles, QTILE), jnp.int32),
            pltpu.VMEM((BLOCK, feat_width), jnp.float32),
        ],
        compiler_params=pltpu.CompilerParams(vmem_limit_bytes=VMEM_LIMIT),
    )(me, owner, local, index_rows, query_all, bias, loss, pos, negs)


def scatter_kernel(
    y_count,
    z_count,
    x_count,
    score_scale,
    part_ref,
    out_ref,
    from_buddy,
    plane_send,
    plane_recv,
    column_send,
    column_recv,
    *sems,
):
    y, core, z, x = coordinates(x_count)
    narrow_count = z_count * x_count
    a_send, a_recv, b_send, b_recv, c_send, c_recv = sems

    def device(dy, other, dz, dx):
        wide = lax.rem(y + dy, y_count) * CORES + (1 - core if other else core)
        return wide, lax.rem(z + dz, z_count) * x_count + lax.rem(x + dx, x_count)

    def number(place):
        return place[0] * narrow_count + place[1]

    def remote(source, target, send_sem, recv_sem, peer):
        return pltpu.make_async_remote_copy(
            src_ref=source,
            dst_ref=target,
            send_sem=send_sem,
            recv_sem=recv_sem,
            device_id=peer,
            device_id_type=MESH,
        )

    shifts = [(dy, dx) for dy in range(y_count) for dx in range(x_count)]
    plane = shifts[1:]
    buddy = device(0, True, 0, 0)
    z_peers = [device(0, False, dz, 0) for dz in range(1, z_count)]
    plane_peers = [device(dy, False, 0, dx) for dy, dx in plane]
    greet(z_peers + plane_peers + [buddy])
    order = [
        (p, dz) for dz in list(range(1, z_count)) + [0] for p in range(1, len(shifts))
    ] + [(0, dz) for dz in list(range(1, z_count)) + [0]]
    to_buddy = {}
    for p, dz in order:
        at = p * z_count + dz
        dy, dx = shifts[p]
        to_buddy[p, dz] = remote(
            part_ref.at[number(device(dy, True, dz, dx))],
            from_buddy.at[at],
            a_send.at[at],
            a_recv.at[at],
            buddy,
        )
        to_buddy[p, dz].start()
    in_plane, held = {}, {}
    for p, dz in order:
        at = p * z_count + dz
        dy, dx = shifts[p]
        to_buddy[p, dz].wait_recv()
        mine = part_ref.at[number(device(dy, False, dz, dx))]
        if p:
            slot = at - z_count
            plane_send[slot] = (mine[...] + from_buddy[at]).astype(jnp.bfloat16)
            in_plane[p, dz] = remote(
                plane_send.at[slot],
                plane_recv.at[slot],
                b_send.at[slot],
                b_recv.at[slot],
                plane_peers[p - 1],
            )
            in_plane[p, dz].start()
    columns = {}
    for dz in list(range(1, z_count)) + [0]:
        total = part_ref.at[number(device(0, False, dz, 0))][...] + from_buddy[dz]
        for p in range(1, len(shifts)):
            in_plane[p, dz].wait_recv()
            total += plane_recv[(p - 1) * z_count + dz].astype(jnp.float32)
        if dz:
            column_send[dz - 1] = total.astype(jnp.bfloat16)
            columns[dz] = remote(
                column_send.at[dz - 1],
                column_recv.at[dz - 1],
                c_send.at[dz - 1],
                c_recv.at[dz - 1],
                z_peers[dz - 1],
            )
            columns[dz].start()
    for dz in range(1, z_count):
        columns[dz].wait_recv()
        total += column_recv[dz - 1].astype(jnp.float32)
    for t in range(total.shape[0]):
        out_ref[t * QTILE : (t + 1) * QTILE, :] = total[t].T * score_scale
    for copy in [*to_buddy.values(), *in_plane.values(), *columns.values()]:
        copy.wait_send()


def scatter_all(partial, counts, score_scale):
    y_count, z_count, x_count = counts
    devices, tiles, feat_width, width = partial.shape
    half = devices // CORES
    passed = half - z_count
    block = (tiles, feat_width, width)
    return pl.pallas_call(
        functools.partial(scatter_kernel, *counts, score_scale),
        out_shape=jax.ShapeDtypeStruct((tiles * width, feat_width), jnp.float32),
        in_specs=[pl.BlockSpec(memory_space=pltpu.VMEM)],
        out_specs=pl.BlockSpec(memory_space=pltpu.VMEM),
        scratch_shapes=[
            pltpu.VMEM((half, *block), jnp.float32),
            pltpu.VMEM((passed, *block), jnp.bfloat16),
            pltpu.VMEM((passed, *block), jnp.bfloat16),
            pltpu.VMEM((z_count - 1, *block), jnp.bfloat16),
            pltpu.VMEM((z_count - 1, *block), jnp.bfloat16),
            pltpu.SemaphoreType.DMA((half,)),
            pltpu.SemaphoreType.DMA((half,)),
            pltpu.SemaphoreType.DMA((passed,)),
            pltpu.SemaphoreType.DMA((passed,)),
            pltpu.SemaphoreType.DMA((z_count - 1,)),
            pltpu.SemaphoreType.DMA((z_count - 1,)),
        ],
        compiler_params=pltpu.CompilerParams(
            collective_id=1, has_side_effects=True, vmem_limit_bytes=VMEM_LIMIT
        ),
    )(partial)


def shards(
    queries, index_rows, lse_shift, loss_weight, positives, tile_negs, fetch_owner, fetch_local
):
    wide_count = lax.axis_size("wide")
    narrow_count = lax.axis_size("narrow")
    devices = wide_count * narrow_count
    counts = place_counts(wide_count, narrow_count)
    narrow_pos = lax.axis_index("narrow")
    feat_width = queries.shape[1]
    own_queries = queries.shape[0]
    fetch_count = fetch_local.shape[0]
    negs_width = tile_negs.shape[1]
    score_scale = 2.0 / math.sqrt(feat_width)

    def share(array):
        length = array.shape[0] // narrow_count
        return lax.dynamic_slice_in_dim(array, narrow_pos * length, length, 0)

    pieces = [
        share(lse_shift),
        share(loss_weight),
        share(positives).astype(jnp.float32),
        share(tile_negs.reshape(-1)).astype(jnp.float32),
        fetch_owner[:, 0].astype(jnp.float32),
        fetch_local.astype(jnp.float32),
    ]
    lengths = [p.shape[0] for p in pieces]
    used = sum(lengths)
    padded = -(-used // (8 * LANES)) * 8 * LANES
    aux = jnp.pad(jnp.concatenate(pieces), (0, padded - used)).reshape(-1, LANES)
    query_all, aux_all = gather_all(queries, aux, counts)
    aux_all = aux_all.reshape(devices, padded)
    unpacked, start = [], 0
    for length in lengths:
        unpacked.append(aux_all[:, start : start + length].reshape(-1))
        start += length
    lse, loss, pos, negs, owner, local = unpacked
    lse_full = lse + math.log(fetch_count * narrow_count * BLOCK)
    bias = ((jnp.log(loss) - lse_full) * math.log2(math.e)).reshape(-1, QTILE)
    me = (lax.axis_index("wide") * narrow_count + narrow_pos).reshape(1)
    partial, index_grad = work(
        me,
        owner.astype(jnp.int32),
        local.astype(jnp.int32),
        index_rows,
        query_all.reshape(-1, feat_width),
        bias,
        loss.reshape(-1, QTILE),
        pos.astype(jnp.int32).reshape(-1, QTILE),
        negs.astype(jnp.int32).reshape(-1, negs_width),
        score_scale,
    )
    tiles = own_queries // QTILE
    query_grad = scatter_all(
        partial.reshape(devices, tiles, feat_width, QTILE), counts, score_scale
    )
    return query_grad, index_grad


def solution(mesh):
    in_specs = (
        P(("wide", "narrow"), None),
        P(("wide", "narrow"), None),
        P("wide"),
        P("wide"),
        P("wide"),
        P("wide", None),
        P(("wide", "narrow"), None),
        P(("wide", "narrow")),
    )
    out_specs = (P(("wide", "narrow"), None), P(("wide", "narrow"), None))
    return jax.shard_map(shards, mesh=mesh, in_specs=in_specs, out_specs=out_specs, check_vma=False)
```

```python
import functools
import math

import jax
import jax.numpy as jnp
from jax import lax
from jax.experimental import pallas as pl
from jax.experimental.pallas import tpu as pltpu
from jax.sharding import PartitionSpec as P

BLOCK = 128
QTILE = 128
CAP = 2
LANES = 128
CORES = 2
MESH = pl.DeviceIdType.MESH
VMEM_LIMIT = 56 * 1024 * 1024
FAR_BELOW = -1e30


def place_counts(wide_count, narrow_count):
    x_count = 1 << (int(math.log2(narrow_count)) // 2)
    return wide_count // CORES, narrow_count // x_count, x_count


def coordinates(x_count):
    wide, narrow = lax.axis_index("wide"), lax.axis_index("narrow")
    return wide // CORES, wide % CORES, narrow // x_count, narrow % x_count


def greet(peers):
    barrier = pltpu.get_barrier_semaphore()
    for peer in peers:
        pl.semaphore_signal(barrier, inc=1, device_id=peer, device_id_type=MESH)
    pl.semaphore_wait(barrier, len(peers))


def gather_kernel(
    y_count,
    z_count,
    x_count,
    query_ref,
    aux_ref,
    index_ref,
    query_all,
    aux_all,
    index_other,
    own_sem,
    index_sem,
    *sems,
):
    y, core, z, x = coordinates(x_count)
    narrow_count = z_count * x_count

    def device(dy, dz, dx):
        wide = lax.rem(y + dy, y_count) * CORES + core
        return wide, lax.rem(z + dz, z_count) * x_count + lax.rem(x + dx, x_count)

    def number(place):
        return place[0] // CORES * narrow_count + place[1]

    plane = [(dy, dx) for dy in range(y_count) for dx in range(x_count)][1:]
    z_peers = [device(0, dz, 0) for dz in range(1, z_count)]
    plane_peers = [device(dy, 0, dx) for dy, dx in plane]
    buddy = (y * CORES + 1 - core, z * x_count + x)
    greet(z_peers + plane_peers + [buddy])
    me = number(device(0, 0, 0))
    pairs = (
        (query_ref, query_all, sems[0], sems[1]),
        (aux_ref, aux_all, sems[2], sems[3]),
    )
    sent = []

    def send(chunk, peer, own):
        for source, whole, send_sem, recv_sem in pairs:
            copy = pltpu.make_async_remote_copy(
                src_ref=source if own else whole.at[chunk],
                dst_ref=whole.at[chunk],
                send_sem=send_sem.at[len(sent) // 2],
                recv_sem=recv_sem.at[chunk],
                device_id=peer,
                device_id_type=MESH,
            )
            copy.start()
            sent.append(copy)

    def arrive(chunk):
        for source, whole, send_sem, recv_sem in pairs:
            pltpu.make_async_remote_copy(
                src_ref=source,
                dst_ref=whole.at[chunk],
                send_sem=send_sem.at[0],
                recv_sem=recv_sem.at[chunk],
                device_id=buddy,
                device_id_type=MESH,
            ).wait_recv()

    for peer in z_peers + plane_peers:
        send(me, peer, True)
    to_buddy = pltpu.make_async_remote_copy(
        src_ref=index_ref,
        dst_ref=index_other,
        send_sem=index_sem.at[0],
        recv_sem=index_sem.at[1],
        device_id=buddy,
        device_id_type=MESH,
    )
    to_buddy.start()
    local = [
        pltpu.make_async_copy(source, whole.at[me], own_sem.at[i])
        for i, (source, whole, _, _) in enumerate(pairs)
    ]
    for copy in local:
        copy.start()
    for dz in range(1, z_count):
        chunk = number(device(0, dz, 0))
        arrive(chunk)
        for peer in plane_peers:
            send(chunk, peer, False)
    for dz in range(z_count):
        for dy, dx in plane:
            arrive(number(device(dy, dz, dx)))
    for copy in sent:
        copy.wait_send()
    for copy in local:
        copy.wait()
    to_buddy.wait()


def gather_all(queries, aux, index_rows, counts):
    y_count, z_count, x_count = counts
    devices = y_count * z_count * x_count
    sends = (z_count - 1) + (y_count * x_count - 1) * z_count
    vmem, anywhere = (pl.BlockSpec(memory_space=m) for m in (pltpu.VMEM, pl.ANY))
    return pl.pallas_call(
        functools.partial(gather_kernel, *counts),
        out_shape=(
            jax.ShapeDtypeStruct((devices, *queries.shape), queries.dtype),
            jax.ShapeDtypeStruct((devices, *aux.shape), aux.dtype),
            jax.ShapeDtypeStruct(index_rows.shape, index_rows.dtype),
        ),
        in_specs=[vmem, vmem, anywhere],
        out_specs=[vmem, vmem, anywhere],
        scratch_shapes=[
            pltpu.SemaphoreType.DMA((2,)),
            pltpu.SemaphoreType.DMA((2,)),
            pltpu.SemaphoreType.DMA((sends,)),
            pltpu.SemaphoreType.DMA((devices,)),
            pltpu.SemaphoreType.DMA((sends,)),
            pltpu.SemaphoreType.DMA((devices,)),
        ],
        compiler_params=pltpu.CompilerParams(
            collective_id=0, has_side_effects=True, vmem_limit_bytes=VMEM_LIMIT
        ),
    )(queries, aux, index_rows)


def work_kernel(
    score_scale,
    groups,
    place_ref,
    owner_ref,
    local_ref,
    index_ref,
    other_ref,
    query_ref,
    bias_ref,
    loss_ref,
    pos_ref,
    negs_ref,
    dq_ref,
    index_grad_ref,
    other_grad_ref,
    slots,
    places,
    index_both,
    grads,
    bias_now,
    rel_now,
    block_sum,
    sems,
):
    group_tiles = bias_ref.shape[0] // groups
    group_slots = owner_ref.shape[0] // groups
    row_count = index_ref.shape[0]
    chunk_tiles = min(4, group_tiles)
    chunk = chunk_tiles * QTILE
    mine, other = place_ref[0], place_ref[1]
    log2_scale = score_scale * math.log2(math.e)
    loads = [
        pltpu.make_async_copy(source, index_both.at[pl.ds(i * row_count, row_count), :], sems.at[i])
        for i, source in enumerate((index_ref, other_ref))
    ]
    for load in loads:
        load.start()
    dq_ref[...] = jnp.zeros_like(dq_ref)
    grads[...] = jnp.zeros_like(grads)
    row_ids = lax.broadcasted_iota(jnp.int32, (BLOCK, QTILE), 0)

    def list_group(group):
        def list_one(slot, count):
            owner = owner_ref[group * group_slots + slot]
            place = local_ref[group * group_slots + slot] * BLOCK
            slots[group, count] = slot
            places[group, count] = place + jnp.where(owner == other, row_count, 0)
            return count + jnp.logical_or(owner == mine, owner == other).astype(jnp.int32)

        count = lax.fori_loop(0, group_slots, list_one, jnp.int32(0), unroll=8)
        slots[group, count] = -1
        places[group, count] = 0
        return count

    counts = [list_group(group) for group in range(groups)]
    for load in loads:
        load.wait()
    for group in range(groups):
        tiles = pl.ds(group * group_tiles, group_tiles)

        @pl.loop(0, (counts[group] + 1) // 2)
        def _(pair):
            rows, blocks, blocks_t = [], [], []
            for h in range(2):
                slot = slots[group, 2 * pair + h]
                place = pl.multiple_of(places[group, 2 * pair + h], BLOCK)
                rows.append(pl.ds(place, BLOCK))
                blocks.append(index_both[rows[h], :])
                blocks_t.append(blocks[h].astype(jnp.float32).T.astype(jnp.bfloat16))
                hit = jnp.any(negs_ref[tiles, :] == slot, axis=1, keepdims=True)
                rel = pos_ref[tiles, :] - slot * BLOCK
                inside = jnp.logical_and(rel >= 0, rel < BLOCK)
                bias_now[h] = jnp.where(
                    jnp.logical_or(hit, inside), bias_ref[tiles, :], FAR_BELOW
                )
                rel_now[h] = rel
            block = jnp.concatenate(blocks, axis=0)
            block_t = jnp.concatenate(blocks_t, axis=1)
            for turn in range(group_tiles // chunk_tiles):
                first = group * group_tiles + turn * chunk_tiles
                query = query_ref[pl.ds(first * QTILE, chunk), :]
                scores = lax.dot_general(
                    block, query, (((1,), (1,)), ((), ())), preferred_element_type=jnp.float32
                )
                halves = []
                for h in range(2):
                    parts = []
                    for t in range(chunk_tiles):
                        at = turn * chunk_tiles + t
                        part = scores[h * BLOCK : (h + 1) * BLOCK, t * QTILE : (t + 1) * QTILE]
                        grown = jnp.exp2(part * log2_scale + bias_now[h, at : at + 1, :])
                        less = grown - loss_ref[first + t : first + t + 1, :]
                        grad = jnp.where(row_ids == rel_now[h, at : at + 1, :], less, grown)
                        parts.append(grad.astype(jnp.bfloat16))
                    halves.append(jnp.concatenate(parts, axis=1))
                logit_grad = jnp.concatenate(halves, axis=0)
                added = jnp.dot(logit_grad, query, preferred_element_type=jnp.float32)
                if turn == 0:
                    block_sum[...] = added
                else:
                    block_sum[...] += added
                part = jnp.dot(block_t, logit_grad, preferred_element_type=jnp.float32)
                for t in range(chunk_tiles):
                    dq_ref[first + t] += part[:, t * QTILE : (t + 1) * QTILE]
            for h in range(2):
                total = block_sum[h * BLOCK : (h + 1) * BLOCK, :] * score_scale
                grads[rows[h], :] += total.astype(jnp.bfloat16).astype(jnp.float32)

    store = pltpu.make_async_copy(grads.at[pl.ds(0, row_count), :], index_grad_ref, sems.at[2])
    store.start()
    other_grad_ref[...] = grads[row_count:, :].astype(jnp.bfloat16)
    store.wait()


def work(place, owner, local, index_rows, index_other, query_all, small, score_scale):
    row_count, feat_width = index_rows.shape
    tile_total = small[0].shape[0]
    groups = lax.axis_size("wide") // CORES
    group_tiles = tile_total // groups
    smem, vmem, anywhere = (
        pl.BlockSpec(memory_space=m) for m in (pltpu.SMEM, pltpu.VMEM, pl.ANY)
    )
    names = (groups, owner.shape[0] // groups + 1)
    return pl.pallas_call(
        functools.partial(work_kernel, score_scale, groups),
        out_shape=(
            jax.ShapeDtypeStruct((tile_total, feat_width, QTILE), jnp.float32),
            jax.ShapeDtypeStruct(index_rows.shape, jnp.float32),
            jax.ShapeDtypeStruct(index_rows.shape, jnp.bfloat16),
        ),
        in_specs=[smem] * 3 + [anywhere] * 2 + [vmem] * 5,
        out_specs=[vmem, anywhere, vmem],
        scratch_shapes=[
            pltpu.SMEM(names, jnp.int32),
            pltpu.SMEM(names, jnp.int32),
            pltpu.VMEM((2 * row_count, feat_width), jnp.bfloat16),
            pltpu.VMEM((2 * row_count, feat_width), jnp.float32),
            pltpu.VMEM((2, group_tiles, QTILE), jnp.float32),
            pltpu.VMEM((2, group_tiles, QTILE), jnp.int32),
            pltpu.VMEM((2 * BLOCK, feat_width), jnp.float32),
            pltpu.SemaphoreType.DMA((3,)),
        ],
        compiler_params=pltpu.CompilerParams(vmem_limit_bytes=VMEM_LIMIT),
    )(place, owner, local, index_rows, index_other, query_all, *small)


def scatter_kernel(
    y_count,
    z_count,
    x_count,
    score_scale,
    part_ref,
    grad_ref,
    out_ref,
    grad_other,
    plane_send,
    plane_recv,
    column_send,
    column_recv,
    a_sem,
    *sems,
):
    y, core, z, x = coordinates(x_count)
    narrow_count = z_count * x_count
    b_send, b_recv, c_send, c_recv = sems

    def device(dy, dz, dx):
        wide = lax.rem(y + dy, y_count) * CORES + core
        return wide, lax.rem(z + dz, z_count) * x_count + lax.rem(x + dx, x_count)

    def number(place):
        return place[0] // CORES * narrow_count + place[1]

    def remote(source, target, send_sem, recv_sem, peer):
        return pltpu.make_async_remote_copy(
            src_ref=source,
            dst_ref=target,
            send_sem=send_sem,
            recv_sem=recv_sem,
            device_id=peer,
            device_id_type=MESH,
        )

    shifts = [(dy, dx) for dy in range(y_count) for dx in range(x_count)]
    buddy = (y * CORES + 1 - core, z * x_count + x)
    z_peers = [device(0, dz, 0) for dz in range(1, z_count)]
    plane_peers = [device(dy, 0, dx) for dy, dx in shifts[1:]]
    greet(z_peers + plane_peers + [buddy])
    z_order = list(range(1, z_count)) + [0]
    to_buddy = remote(grad_ref, grad_other, a_sem.at[0], a_sem.at[1], buddy)
    to_buddy.start()
    in_plane, columns = {}, {}
    for dz in z_order:
        for p in range(1, len(shifts)):
            slot = (p - 1) * z_count + dz
            dy, dx = shifts[p]
            plane_send[slot] = part_ref[number(device(dy, dz, dx))].astype(jnp.bfloat16)
            in_plane[p, dz] = remote(
                plane_send.at[slot],
                plane_recv.at[slot],
                b_send.at[slot],
                b_recv.at[slot],
                plane_peers[p - 1],
            )
            in_plane[p, dz].start()
    for dz in z_order:
        total = part_ref[number(device(0, dz, 0))]
        for p in range(1, len(shifts)):
            in_plane[p, dz].wait_recv()
            total += plane_recv[(p - 1) * z_count + dz].astype(jnp.float32)
        if dz:
            column_send[dz - 1] = total.astype(jnp.bfloat16)
            columns[dz] = remote(
                column_send.at[dz - 1],
                column_recv.at[dz - 1],
                c_send.at[dz - 1],
                c_recv.at[dz - 1],
                z_peers[dz - 1],
            )
            columns[dz].start()
    for dz in range(1, z_count):
        columns[dz].wait_recv()
        total += column_recv[dz - 1].astype(jnp.float32)
    for t in range(total.shape[0]):
        out_ref[t * QTILE : (t + 1) * QTILE, :] = total[t].T * score_scale
    for copy in [*in_plane.values(), *columns.values()]:
        copy.wait_send()
    to_buddy.wait()


def scatter_all(partial, other_grad, counts, score_scale):
    y_count, z_count, x_count = counts
    devices, tiles, feat_width, width = partial.shape
    passed = devices - z_count
    block = (tiles, feat_width, width)
    vmem, anywhere = (pl.BlockSpec(memory_space=m) for m in (pltpu.VMEM, pl.ANY))
    return pl.pallas_call(
        functools.partial(scatter_kernel, *counts, score_scale),
        out_shape=(
            jax.ShapeDtypeStruct((tiles * width, feat_width), jnp.float32),
            jax.ShapeDtypeStruct(other_grad.shape, other_grad.dtype),
        ),
        in_specs=[vmem, anywhere],
        out_specs=[vmem, anywhere],
        scratch_shapes=[
            pltpu.VMEM((passed, *block), jnp.bfloat16),
            pltpu.VMEM((passed, *block), jnp.bfloat16),
            pltpu.VMEM((z_count - 1, *block), jnp.bfloat16),
            pltpu.VMEM((z_count - 1, *block), jnp.bfloat16),
            pltpu.SemaphoreType.DMA((2,)),
            pltpu.SemaphoreType.DMA((passed,)),
            pltpu.SemaphoreType.DMA((passed,)),
            pltpu.SemaphoreType.DMA((z_count - 1,)),
            pltpu.SemaphoreType.DMA((z_count - 1,)),
        ],
        compiler_params=pltpu.CompilerParams(
            collective_id=1, has_side_effects=True, vmem_limit_bytes=VMEM_LIMIT
        ),
    )(partial, other_grad)


def shards(
    queries, index_rows, lse_shift, loss_weight, positives, tile_negs, fetch_owner, fetch_local
):
    wide_count = lax.axis_size("wide")
    narrow_count = lax.axis_size("narrow")
    devices = wide_count // CORES * narrow_count
    counts = place_counts(wide_count, narrow_count)
    narrow_pos = lax.axis_index("narrow")
    feat_width = queries.shape[1]
    own_queries = queries.shape[0]
    fetch_count = fetch_local.shape[0]
    negs_width = tile_negs.shape[1]
    score_scale = 2.0 / math.sqrt(feat_width)

    def share(array):
        length = array.shape[0] // narrow_count
        return lax.dynamic_slice_in_dim(array, narrow_pos * length, length, 0)

    pieces = [
        share(lse_shift),
        share(loss_weight),
        share(positives).astype(jnp.float32),
        share(tile_negs.reshape(-1)).astype(jnp.float32),
        fetch_owner[:, 0].astype(jnp.float32),
        fetch_local.astype(jnp.float32),
    ]
    lengths = [p.shape[0] for p in pieces]
    used = sum(lengths)
    padded = -(-used // (8 * LANES)) * 8 * LANES
    aux = jnp.pad(jnp.concatenate(pieces), (0, padded - used)).reshape(-1, LANES)
    query_all, aux_all, index_other = gather_all(queries, aux, index_rows, counts)
    aux_all = aux_all.reshape(devices, padded)
    unpacked, start = [], 0
    for length in lengths:
        unpacked.append(aux_all[:, start : start + length].reshape(-1))
        start += length
    lse, loss, pos, negs, owner, local = unpacked
    lse_full = lse + math.log(fetch_count * narrow_count * BLOCK)
    bias = ((jnp.log(loss) - lse_full) * math.log2(math.e)).reshape(-1, QTILE)
    wide_pos = lax.axis_index("wide")
    buddy_pos = wide_pos + 1 - 2 * (wide_pos % CORES)
    place = jnp.stack([wide_pos * narrow_count + narrow_pos, buddy_pos * narrow_count + narrow_pos])
    small = (
        bias,
        loss.reshape(-1, QTILE),
        pos.astype(jnp.int32).reshape(-1, QTILE),
        negs.astype(jnp.int32).reshape(-1, negs_width),
    )
    partial, index_grad, other_grad = work(
        place,
        owner.astype(jnp.int32),
        local.astype(jnp.int32),
        index_rows,
        index_other,
        query_all.reshape(-1, feat_width),
        small,
        score_scale,
    )
    tiles = own_queries // QTILE
    query_grad, more_grad = scatter_all(
        partial.reshape(devices, tiles, feat_width, QTILE), other_grad, counts, score_scale
    )
    return query_grad, index_grad + more_grad.astype(jnp.float32)


def solution(mesh):
    in_specs = (
        P(("wide", "narrow"), None),
        P(("wide", "narrow"), None),
        P("wide"),
        P("wide"),
        P("wide"),
        P("wide", None),
        P(("wide", "narrow"), None),
        P(("wide", "narrow")),
    )
    out_specs = (P(("wide", "narrow"), None), P(("wide", "narrow"), None))
    return jax.shard_map(shards, mesh=mesh, in_specs=in_specs, out_specs=out_specs, check_vma=False)
```

```python
import functools
import math

import jax
import jax.numpy as jnp
from jax import lax
from jax.experimental import pallas as pl
from jax.experimental.pallas import tpu as pltpu
from jax.sharding import PartitionSpec as P

BLOCK = 128
QTILE = 128
CAP = 2
LANES = 128
CORES = 2
MESH = pl.DeviceIdType.MESH
VMEM_LIMIT = 56 * 1024 * 1024
FAR_BELOW = -1e30


def place_counts(wide_count, narrow_count):
    x_count = 1 << (int(math.log2(narrow_count)) // 2)
    return wide_count // CORES, narrow_count // x_count, x_count


def coordinates(x_count):
    wide, narrow = lax.axis_index("wide"), lax.axis_index("narrow")
    return wide // CORES, wide % CORES, narrow // x_count, narrow % x_count


def greet(peers):
    barrier = pltpu.get_barrier_semaphore()
    for peer in peers:
        pl.semaphore_signal(barrier, inc=1, device_id=peer, device_id_type=MESH)
    pl.semaphore_wait(barrier, len(peers))


def gather_kernel(
    y_count,
    z_count,
    x_count,
    query_ref,
    aux_ref,
    index_ref,
    *refs,
):
    kinds = (len(refs) - 10) // 2
    small = refs[:kinds]
    query_all, aux_all, index_other = refs[kinds : kinds + 3]
    small_all = refs[kinds + 3 : 2 * kinds + 3]
    own_sem, index_sem, small_sem, *sems = refs[2 * kinds + 3 :]
    y, core, z, x = coordinates(x_count)
    narrow_count = z_count * x_count

    def device(dy, dz, dx):
        wide = lax.rem(y + dy, y_count) * CORES + core
        return wide, lax.rem(z + dz, z_count) * x_count + lax.rem(x + dx, x_count)

    def number(place):
        return place[0] // CORES * narrow_count + place[1]

    plane = [(dy, dx) for dy in range(y_count) for dx in range(x_count)][1:]
    z_peers = [device(0, dz, 0) for dz in range(1, z_count)]
    plane_peers = [device(dy, 0, dx) for dy, dx in plane]
    buddy = (y * CORES + 1 - core, z * x_count + x)
    greet(z_peers + plane_peers + [buddy])
    me = number(device(0, 0, 0))
    pairs = (
        (query_ref, query_all, sems[0], sems[1]),
        (aux_ref, aux_all, sems[2], sems[3]),
    )
    sent = []

    def send(chunk, peer, own):
        for source, whole, send_sem, recv_sem in pairs:
            copy = pltpu.make_async_remote_copy(
                src_ref=source if own else whole.at[chunk],
                dst_ref=whole.at[chunk],
                send_sem=send_sem.at[len(sent) // 2],
                recv_sem=recv_sem.at[chunk],
                device_id=peer,
                device_id_type=MESH,
            )
            copy.start()
            sent.append(copy)

    def arrive(chunk):
        for source, whole, send_sem, recv_sem in pairs:
            pltpu.make_async_remote_copy(
                src_ref=source,
                dst_ref=whole.at[chunk],
                send_sem=send_sem.at[0],
                recv_sem=recv_sem.at[chunk],
                device_id=buddy,
                device_id_type=MESH,
            ).wait_recv()

    for peer in z_peers + plane_peers:
        send(me, peer, True)
    to_buddy = pltpu.make_async_remote_copy(
        src_ref=index_ref,
        dst_ref=index_other,
        send_sem=index_sem.at[0],
        recv_sem=index_sem.at[1],
        device_id=buddy,
        device_id_type=MESH,
    )
    to_buddy.start()
    groups = []
    for dy in range(1, y_count):
        for i in range(kinds):
            groups.append(
                pltpu.make_async_remote_copy(
                    src_ref=small[i],
                    dst_ref=small_all[i].at[y],
                    send_sem=small_sem.at[0, i, dy],
                    recv_sem=small_sem.at[1, i, dy],
                    device_id=device(dy, 0, 0),
                    device_id_type=MESH,
                )
            )
            groups[-1].start()
    local = [
        pltpu.make_async_copy(source, target, own_sem.at[i])
        for i, (source, target) in enumerate(
            [(query_ref, query_all.at[me]), (aux_ref, aux_all.at[me])]
            + [(small[i], small_all[i].at[y]) for i in range(kinds)]
        )
    ]
    for copy in local:
        copy.start()
    for dz in range(1, z_count):
        chunk = number(device(0, dz, 0))
        arrive(chunk)
        for peer in plane_peers:
            send(chunk, peer, False)
    for dz in range(z_count):
        for dy, dx in plane:
            arrive(number(device(dy, dz, dx)))
    for copy in sent:
        copy.wait_send()
    for copy in local:
        copy.wait()
    for copy in groups:
        copy.wait()
    to_buddy.wait()


def gather_all(queries, aux, index_rows, small, counts):
    y_count, z_count, x_count = counts
    devices = y_count * z_count * x_count
    sends = (z_count - 1) + (y_count * x_count - 1) * z_count
    vmem, anywhere = (pl.BlockSpec(memory_space=m) for m in (pltpu.VMEM, pl.ANY))
    return pl.pallas_call(
        functools.partial(gather_kernel, *counts),
        out_shape=(
            jax.ShapeDtypeStruct((devices, *queries.shape), queries.dtype),
            jax.ShapeDtypeStruct((devices, *aux.shape), aux.dtype),
            jax.ShapeDtypeStruct(index_rows.shape, index_rows.dtype),
            *(jax.ShapeDtypeStruct((y_count, *a.shape), a.dtype) for a in small),
        ),
        in_specs=[vmem, vmem, anywhere] + [vmem] * len(small),
        out_specs=[vmem, vmem, anywhere] + [vmem] * len(small),
        scratch_shapes=[
            pltpu.SemaphoreType.DMA((2 + len(small),)),
            pltpu.SemaphoreType.DMA((2,)),
            pltpu.SemaphoreType.DMA((2, len(small), y_count)),
            pltpu.SemaphoreType.DMA((sends,)),
            pltpu.SemaphoreType.DMA((devices,)),
            pltpu.SemaphoreType.DMA((sends,)),
            pltpu.SemaphoreType.DMA((devices,)),
        ],
        compiler_params=pltpu.CompilerParams(
            collective_id=0, has_side_effects=True, vmem_limit_bytes=VMEM_LIMIT
        ),
    )(queries, aux, index_rows, *small)


def work_kernel(
    score_scale,
    groups,
    fetch_count,
    place_ref,
    fetch_ref,
    index_ref,
    other_ref,
    query_ref,
    lse_ref,
    loss_ref,
    pos_ref,
    negs_ref,
    dq_ref,
    index_grad_ref,
    other_grad_ref,
    slots,
    places,
    index_both,
    grads,
    bias_now,
    rel_now,
    block_sum,
    bias_all,
    sems,
):
    group_tiles = lse_ref.shape[1]
    narrow_count = fetch_ref.shape[0] // groups
    log_total = math.log(fetch_count * narrow_count * BLOCK)
    row_count = index_ref.shape[0]
    chunk_tiles = min(4, group_tiles)
    chunk = chunk_tiles * QTILE
    mine, other = place_ref[0], place_ref[1]
    log2_scale = score_scale * math.log2(math.e)
    loads = [
        pltpu.make_async_copy(source, index_both.at[pl.ds(i * row_count, row_count), :], sems.at[i])
        for i, source in enumerate((index_ref, other_ref))
    ]
    for load in loads:
        load.start()
    dq_ref[...] = jnp.zeros_like(dq_ref)
    grads[...] = jnp.zeros_like(grads)
    row_ids = lax.broadcasted_iota(jnp.int32, (BLOCK, QTILE), 0)

    bias_all[...] = (jnp.log(loss_ref[...]) - (lse_ref[...] + log_total)) * math.log2(math.e)

    def list_group(group):
        def list_device(device, count):
            for j in range(fetch_count):
                owner = fetch_ref[group * narrow_count + device, 0, j]
                place = fetch_ref[group * narrow_count + device, 0, fetch_count + j] * BLOCK
                slots[group, count] = device * fetch_count + j
                places[group, count] = place + jnp.where(owner == other, row_count, 0)
                count += jnp.logical_or(owner == mine, owner == other).astype(jnp.int32)
            return count

        count = lax.fori_loop(0, narrow_count, list_device, jnp.int32(0))
        slots[group, count] = -1
        places[group, count] = 0
        return count

    counts = [list_group(group) for group in range(groups)]
    for load in loads:
        load.wait()
    for group in range(groups):
        @pl.loop(0, (counts[group] + 1) // 2)
        def _(pair):
            rows, blocks, blocks_t = [], [], []
            for h in range(2):
                slot = slots[group, 2 * pair + h]
                place = pl.multiple_of(places[group, 2 * pair + h], BLOCK)
                rows.append(pl.ds(place, BLOCK))
                blocks.append(index_both[rows[h], :])
                blocks_t.append(blocks[h].astype(jnp.float32).T.astype(jnp.bfloat16))
                hit = jnp.any(negs_ref[group] == slot, axis=1, keepdims=True)
                rel = pos_ref[group] - slot * BLOCK
                inside = jnp.logical_and(rel >= 0, rel < BLOCK)
                bias_now[h] = jnp.where(
                    jnp.logical_or(hit, inside), bias_all[group], FAR_BELOW
                )
                rel_now[h] = rel
            block = jnp.concatenate(blocks, axis=0)
            block_t = jnp.concatenate(blocks_t, axis=1)
            turns = group_tiles // chunk_tiles

            def load(turn):
                first = (group * group_tiles + turn * chunk_tiles) * QTILE
                return query_ref[pl.ds(first, chunk), :]

            def score(turn):
                return lax.dot_general(
                    block, load(turn), (((1,), (1,)), ((), ())), preferred_element_type=jnp.float32
                )

            def grad_of(turn, scores):
                halves = []
                for h in range(2):
                    parts = []
                    for t in range(chunk_tiles):
                        at = slice(turn * chunk_tiles + t, turn * chunk_tiles + t + 1)
                        part = scores[h * BLOCK : (h + 1) * BLOCK, t * QTILE : (t + 1) * QTILE]
                        grown = jnp.exp2(part * log2_scale + bias_now[h, at, :])
                        less = grown - loss_ref[group, at, :]
                        grad = jnp.where(row_ids == rel_now[h, at, :], less, grown)
                        parts.append(grad.astype(jnp.bfloat16))
                    halves.append(jnp.concatenate(parts, axis=1))
                return jnp.concatenate(halves, axis=0)

            def add(turn, logit_grad):
                first = group * group_tiles + turn * chunk_tiles
                added = jnp.dot(logit_grad, load(turn), preferred_element_type=jnp.float32)
                if turn == 0:
                    block_sum[...] = added
                else:
                    block_sum[...] += added
                part = jnp.dot(block_t, logit_grad, preferred_element_type=jnp.float32)
                for t in range(chunk_tiles):
                    dq_ref[first + t] += part[:, t * QTILE : (t + 1) * QTILE]

            scores, before = score(0), None
            for turn in range(turns):
                ahead = score(turn + 1) if turn + 1 < turns else None
                if turn:
                    add(turn - 1, before)
                before = grad_of(turn, scores)
                scores = ahead
            add(turns - 1, before)
            for h in range(2):
                total = block_sum[h * BLOCK : (h + 1) * BLOCK, :] * score_scale
                grads[rows[h], :] += total.astype(jnp.bfloat16).astype(jnp.float32)

    store = pltpu.make_async_copy(grads.at[pl.ds(0, row_count), :], index_grad_ref, sems.at[2])
    store.start()
    other_grad_ref[...] = grads[row_count:, :].astype(jnp.bfloat16)
    store.wait()


def work(place, fetch_all, index_rows, index_other, query_all, small, fetch_count, score_scale):
    row_count, feat_width = index_rows.shape
    groups, group_tiles, _ = small[0].shape
    tile_total = groups * group_tiles
    smem, vmem, anywhere = (
        pl.BlockSpec(memory_space=m) for m in (pltpu.SMEM, pltpu.VMEM, pl.ANY)
    )
    names = (groups, fetch_all.shape[0] // groups * fetch_count + 1)
    return pl.pallas_call(
        functools.partial(work_kernel, score_scale, groups, fetch_count),
        out_shape=(
            jax.ShapeDtypeStruct((tile_total, feat_width, QTILE), jnp.float32),
            jax.ShapeDtypeStruct(index_rows.shape, jnp.float32),
            jax.ShapeDtypeStruct(index_rows.shape, jnp.bfloat16),
        ),
        in_specs=[smem] * 2 + [anywhere] * 2 + [vmem] * 5,
        out_specs=[vmem, anywhere, vmem],
        scratch_shapes=[
            pltpu.SMEM(names, jnp.int32),
            pltpu.SMEM(names, jnp.int32),
            pltpu.VMEM((2 * row_count, feat_width), jnp.bfloat16),
            pltpu.VMEM((2 * row_count, feat_width), jnp.float32),
            pltpu.VMEM((2, group_tiles, QTILE), jnp.float32),
            pltpu.VMEM((2, group_tiles, QTILE), jnp.int32),
            pltpu.VMEM((2 * BLOCK, feat_width), jnp.float32),
            pltpu.VMEM((groups, group_tiles, QTILE), jnp.float32),
            pltpu.SemaphoreType.DMA((3,)),
        ],
        compiler_params=pltpu.CompilerParams(vmem_limit_bytes=VMEM_LIMIT),
    )(place, fetch_all, index_rows, index_other, query_all, *small)


def scatter_kernel(
    y_count,
    z_count,
    x_count,
    score_scale,
    part_ref,
    grad_ref,
    out_ref,
    grad_other,
    plane_send,
    plane_recv,
    column_send,
    column_recv,
    a_sem,
    *sems,
):
    y, core, z, x = coordinates(x_count)
    narrow_count = z_count * x_count
    b_send, b_recv, c_send, c_recv = sems

    def device(dy, dz, dx):
        wide = lax.rem(y + dy, y_count) * CORES + core
        return wide, lax.rem(z + dz, z_count) * x_count + lax.rem(x + dx, x_count)

    def number(place):
        return place[0] // CORES * narrow_count + place[1]

    def remote(source, target, send_sem, recv_sem, peer):
        return pltpu.make_async_remote_copy(
            src_ref=source,
            dst_ref=target,
            send_sem=send_sem,
            recv_sem=recv_sem,
            device_id=peer,
            device_id_type=MESH,
        )

    shifts = [(dy, dx) for dy in range(y_count) for dx in range(x_count)]
    buddy = (y * CORES + 1 - core, z * x_count + x)
    z_peers = [device(0, dz, 0) for dz in range(1, z_count)]
    plane_peers = [device(dy, 0, dx) for dy, dx in shifts[1:]]
    greet(z_peers + plane_peers + [buddy])
    z_order = list(range(1, z_count)) + [0]
    to_buddy = remote(grad_ref, grad_other, a_sem.at[0], a_sem.at[1], buddy)
    to_buddy.start()
    in_plane, columns = {}, {}
    for dz in z_order:
        for p in range(1, len(shifts)):
            slot = (p - 1) * z_count + dz
            dy, dx = shifts[p]
            plane_send[slot] = part_ref[number(device(dy, dz, dx))].astype(jnp.bfloat16)
            in_plane[p, dz] = remote(
                plane_send.at[slot],
                plane_recv.at[slot],
                b_send.at[slot],
                b_recv.at[slot],
                plane_peers[p - 1],
            )
            in_plane[p, dz].start()
    for dz in z_order:
        total = part_ref[number(device(0, dz, 0))]
        for p in range(1, len(shifts)):
            in_plane[p, dz].wait_recv()
            total += plane_recv[(p - 1) * z_count + dz].astype(jnp.float32)
        if dz:
            column_send[dz - 1] = total.astype(jnp.bfloat16)
            columns[dz] = remote(
                column_send.at[dz - 1],
                column_recv.at[dz - 1],
                c_send.at[dz - 1],
                c_recv.at[dz - 1],
                z_peers[dz - 1],
            )
            columns[dz].start()
    for dz in range(1, z_count):
        columns[dz].wait_recv()
        total += column_recv[dz - 1].astype(jnp.float32)
    for t in range(total.shape[0]):
        out_ref[t * QTILE : (t + 1) * QTILE, :] = total[t].T * score_scale
    for copy in [*in_plane.values(), *columns.values()]:
        copy.wait_send()
    to_buddy.wait()


def scatter_all(partial, other_grad, counts, score_scale):
    y_count, z_count, x_count = counts
    devices, tiles, feat_width, width = partial.shape
    passed = devices - z_count
    block = (tiles, feat_width, width)
    vmem, anywhere = (pl.BlockSpec(memory_space=m) for m in (pltpu.VMEM, pl.ANY))
    return pl.pallas_call(
        functools.partial(scatter_kernel, *counts, score_scale),
        out_shape=(
            jax.ShapeDtypeStruct((tiles * width, feat_width), jnp.float32),
            jax.ShapeDtypeStruct(other_grad.shape, other_grad.dtype),
        ),
        in_specs=[vmem, anywhere],
        out_specs=[vmem, anywhere],
        scratch_shapes=[
            pltpu.VMEM((passed, *block), jnp.bfloat16),
            pltpu.VMEM((passed, *block), jnp.bfloat16),
            pltpu.VMEM((z_count - 1, *block), jnp.bfloat16),
            pltpu.VMEM((z_count - 1, *block), jnp.bfloat16),
            pltpu.SemaphoreType.DMA((2,)),
            pltpu.SemaphoreType.DMA((passed,)),
            pltpu.SemaphoreType.DMA((passed,)),
            pltpu.SemaphoreType.DMA((z_count - 1,)),
            pltpu.SemaphoreType.DMA((z_count - 1,)),
        ],
        compiler_params=pltpu.CompilerParams(
            collective_id=1, has_side_effects=True, vmem_limit_bytes=VMEM_LIMIT
        ),
    )(partial, other_grad)


def shards(
    queries, index_rows, lse_shift, loss_weight, positives, tile_negs, fetch_owner, fetch_local
):
    wide_count = lax.axis_size("wide")
    narrow_count = lax.axis_size("narrow")
    devices = wide_count // CORES * narrow_count
    counts = place_counts(wide_count, narrow_count)
    narrow_pos = lax.axis_index("narrow")
    feat_width = queries.shape[1]
    own_queries = queries.shape[0]
    fetch_count = fetch_local.shape[0]
    score_scale = 2.0 / math.sqrt(feat_width)
    named = jnp.concatenate([fetch_owner[:, 0], fetch_local])
    padded = -(-2 * fetch_count // LANES) * LANES
    named = jnp.pad(named, (0, padded - 2 * fetch_count)).reshape(1, padded)
    small = [a.reshape(-1, QTILE) for a in (lse_shift, loss_weight, positives)] + [tile_negs]
    query_all, fetch_all, index_other, *small = gather_all(
        queries, named, index_rows, small, counts
    )
    wide_pos = lax.axis_index("wide")
    buddy_pos = wide_pos + 1 - 2 * (wide_pos % CORES)
    place = jnp.stack([wide_pos * narrow_count + narrow_pos, buddy_pos * narrow_count + narrow_pos])
    partial, index_grad, other_grad = work(
        place,
        fetch_all,
        index_rows,
        index_other,
        query_all.reshape(-1, feat_width),
        small,
        fetch_count,
        score_scale,
    )
    tiles = own_queries // QTILE
    query_grad, more_grad = scatter_all(
        partial.reshape(devices, tiles, feat_width, QTILE), other_grad, counts, score_scale
    )
    return query_grad, index_grad + more_grad.astype(jnp.float32)


def solution(mesh):
    in_specs = (
        P(("wide", "narrow"), None),
        P(("wide", "narrow"), None),
        P("wide"),
        P("wide"),
        P("wide"),
        P("wide", None),
        P(("wide", "narrow"), None),
        P(("wide", "narrow")),
    )
    out_specs = (P(("wide", "narrow"), None), P(("wide", "narrow"), None))
    return jax.shard_map(shards, mesh=mesh, in_specs=in_specs, out_specs=out_specs, check_vma=False)
```

```python
import functools
import math

import jax
import jax.numpy as jnp
from jax import lax
from jax.experimental import pallas as pl
from jax.experimental.pallas import tpu as pltpu
from jax.sharding import PartitionSpec as P

BLOCK = 128
QTILE = 128
CAP = 2
LANES = 128
CORES = 2
TOGETHER = 4
MESH = pl.DeviceIdType.MESH
VMEM_LIMIT = 56 * 1024 * 1024
FAR_BELOW = -1e30


def place_counts(wide_count, narrow_count):
    x_count = 1 << (int(math.log2(narrow_count)) // 2)
    return wide_count // CORES, narrow_count // x_count, x_count


def coordinates(x_count):
    wide, narrow = lax.axis_index("wide"), lax.axis_index("narrow")
    return wide // CORES, wide % CORES, narrow // x_count, narrow % x_count


def greet(peers):
    barrier = pltpu.get_barrier_semaphore()
    for peer in peers:
        pl.semaphore_signal(barrier, inc=1, device_id=peer, device_id_type=MESH)
    pl.semaphore_wait(barrier, len(peers))


def gather_kernel(
    y_count,
    z_count,
    x_count,
    query_ref,
    aux_ref,
    index_ref,
    *refs,
):
    kinds = (len(refs) - 10) // 2
    small = refs[:kinds]
    query_all, aux_all, index_other = refs[kinds : kinds + 3]
    small_all = refs[kinds + 3 : 2 * kinds + 3]
    own_sem, index_sem, small_sem, *sems = refs[2 * kinds + 3 :]
    y, core, z, x = coordinates(x_count)
    narrow_count = z_count * x_count

    def device(dy, dz, dx):
        wide = lax.rem(y + dy, y_count) * CORES + core
        return wide, lax.rem(z + dz, z_count) * x_count + lax.rem(x + dx, x_count)

    def number(place):
        return place[0] // CORES * narrow_count + place[1]

    plane = [(dy, dx) for dy in range(y_count) for dx in range(x_count)][1:]
    z_peers = [device(0, dz, 0) for dz in range(1, z_count)]
    plane_peers = [device(dy, 0, dx) for dy, dx in plane]
    buddy = (y * CORES + 1 - core, z * x_count + x)
    greet(z_peers + plane_peers + [buddy])
    me = number(device(0, 0, 0))
    pairs = (
        (query_ref, query_all, sems[0], sems[1]),
        (aux_ref, aux_all, sems[2], sems[3]),
    )
    sent = []

    def send(chunk, peer, own):
        for source, whole, send_sem, recv_sem in pairs:
            copy = pltpu.make_async_remote_copy(
                src_ref=source if own else whole.at[chunk],
                dst_ref=whole.at[chunk],
                send_sem=send_sem.at[len(sent) // 2],
                recv_sem=recv_sem.at[chunk],
                device_id=peer,
                device_id_type=MESH,
            )
            copy.start()
            sent.append(copy)

    def arrive(chunk):
        for source, whole, send_sem, recv_sem in pairs:
            pltpu.make_async_remote_copy(
                src_ref=source,
                dst_ref=whole.at[chunk],
                send_sem=send_sem.at[0],
                recv_sem=recv_sem.at[chunk],
                device_id=buddy,
                device_id_type=MESH,
            ).wait_recv()

    for peer in z_peers + plane_peers:
        send(me, peer, True)
    to_buddy = pltpu.make_async_remote_copy(
        src_ref=index_ref,
        dst_ref=index_other,
        send_sem=index_sem.at[0],
        recv_sem=index_sem.at[1],
        device_id=buddy,
        device_id_type=MESH,
    )
    to_buddy.start()
    groups = []
    for dy in range(1, y_count):
        for i in range(kinds):
            groups.append(
                pltpu.make_async_remote_copy(
                    src_ref=small[i],
                    dst_ref=small_all[i].at[y],
                    send_sem=small_sem.at[0, i, dy],
                    recv_sem=small_sem.at[1, i, dy],
                    device_id=device(dy, 0, 0),
                    device_id_type=MESH,
                )
            )
            groups[-1].start()
    local = [
        pltpu.make_async_copy(source, target, own_sem.at[i])
        for i, (source, target) in enumerate(
            [(query_ref, query_all.at[me]), (aux_ref, aux_all.at[me])]
            + [(small[i], small_all[i].at[y]) for i in range(kinds)]
        )
    ]
    for copy in local:
        copy.start()
    for dz in range(1, z_count):
        chunk = number(device(0, dz, 0))
        arrive(chunk)
        for peer in plane_peers:
            send(chunk, peer, False)
    for dz in range(z_count):
        for dy, dx in plane:
            arrive(number(device(dy, dz, dx)))
    for copy in sent:
        copy.wait_send()
    for copy in local:
        copy.wait()
    for copy in groups:
        copy.wait()
    to_buddy.wait()


def gather_all(queries, aux, index_rows, small, counts):
    y_count, z_count, x_count = counts
    devices = y_count * z_count * x_count
    sends = (z_count - 1) + (y_count * x_count - 1) * z_count
    vmem, anywhere = (pl.BlockSpec(memory_space=m) for m in (pltpu.VMEM, pl.ANY))
    return pl.pallas_call(
        functools.partial(gather_kernel, *counts),
        out_shape=(
            jax.ShapeDtypeStruct((devices, *queries.shape), queries.dtype),
            jax.ShapeDtypeStruct((devices, *aux.shape), aux.dtype),
            jax.ShapeDtypeStruct(index_rows.shape, index_rows.dtype),
            *(jax.ShapeDtypeStruct((y_count, *a.shape), a.dtype) for a in small),
        ),
        in_specs=[vmem, vmem, anywhere] + [vmem] * len(small),
        out_specs=[vmem, vmem, anywhere] + [vmem] * len(small),
        scratch_shapes=[
            pltpu.SemaphoreType.DMA((2 + len(small),)),
            pltpu.SemaphoreType.DMA((2,)),
            pltpu.SemaphoreType.DMA((2, len(small), y_count)),
            pltpu.SemaphoreType.DMA((sends,)),
            pltpu.SemaphoreType.DMA((devices,)),
            pltpu.SemaphoreType.DMA((sends,)),
            pltpu.SemaphoreType.DMA((devices,)),
        ],
        compiler_params=pltpu.CompilerParams(
            collective_id=0, has_side_effects=True, vmem_limit_bytes=VMEM_LIMIT
        ),
    )(queries, aux, index_rows, *small)


def work_kernel(
    score_scale,
    groups,
    fetch_count,
    fetch_ref,
    index_ref,
    other_ref,
    query_ref,
    lse_ref,
    loss_ref,
    pos_ref,
    negs_ref,
    dq_ref,
    index_grad_ref,
    other_grad_ref,
    slots,
    places,
    index_both,
    grads,
    bias_now,
    rel_now,
    block_sum,
    bias_all,
    sems,
):
    group_tiles = lse_ref.shape[1]
    narrow_count = fetch_ref.shape[0] // groups
    log_total = math.log(fetch_count * narrow_count * BLOCK)
    row_count = index_ref.shape[0]
    chunk_tiles = min(4, group_tiles)
    chunk = chunk_tiles * QTILE
    wide, narrow = lax.axis_index("wide"), lax.axis_index("narrow")
    mine = wide * narrow_count + narrow
    other = (wide // CORES * CORES + 1 - wide % CORES) * narrow_count + narrow
    log2_scale = score_scale * math.log2(math.e)
    loads = [
        pltpu.make_async_copy(source, index_both.at[pl.ds(i * row_count, row_count), :], sems.at[i])
        for i, source in enumerate((index_ref, other_ref))
    ]
    for load in loads:
        load.start()
    dq_ref[...] = jnp.zeros_like(dq_ref)
    grads[...] = jnp.zeros_like(grads)
    row_ids = lax.broadcasted_iota(jnp.int32, (BLOCK, QTILE), 0)

    bias_all[...] = (jnp.log(loss_ref[...]) - (lse_ref[...] + log_total)) * math.log2(math.e)

    def list_group(group):
        def list_device(device, count):
            for j in range(fetch_count):
                owner = fetch_ref[group * narrow_count + device, 0, j]
                place = fetch_ref[group * narrow_count + device, 0, fetch_count + j] * BLOCK
                slots[group, count] = device * fetch_count + j
                places[group, count] = place + jnp.where(owner == other, row_count, 0)
                count += jnp.logical_or(owner == mine, owner == other).astype(jnp.int32)
            return count

        count = lax.fori_loop(0, narrow_count, list_device, jnp.int32(0))
        for extra in range(TOGETHER - 1):
            slots[group, count + extra] = -1
            places[group, count + extra] = 0
        return count

    counts = [list_group(group) for group in range(groups)]
    for load in loads:
        load.wait()
    for group in range(groups):
        @pl.loop(0, (counts[group] + TOGETHER - 1) // TOGETHER)
        def _(turn_of):
            rows, blocks, blocks_t = [], [], []
            for h in range(TOGETHER):
                slot = slots[group, TOGETHER * turn_of + h]
                place = pl.multiple_of(places[group, TOGETHER * turn_of + h], BLOCK)
                rows.append(pl.ds(place, BLOCK))
                blocks.append(index_both[rows[h], :])
                blocks_t.append(blocks[h].astype(jnp.float32).T.astype(jnp.bfloat16))
                hit = jnp.any(negs_ref[group] == slot, axis=1, keepdims=True)
                rel = pos_ref[group] - slot * BLOCK
                inside = jnp.logical_and(rel >= 0, rel < BLOCK)
                bias_now[h] = jnp.where(
                    jnp.logical_or(hit, inside), bias_all[group], FAR_BELOW
                )
                rel_now[h] = rel
            block = jnp.concatenate(blocks, axis=0)
            block_t = jnp.concatenate(blocks_t, axis=1)
            turns = group_tiles // chunk_tiles

            def load(turn):
                first = (group * group_tiles + turn * chunk_tiles) * QTILE
                return query_ref[pl.ds(first, chunk), :]

            def score(turn):
                return lax.dot_general(
                    block, load(turn), (((1,), (1,)), ((), ())), preferred_element_type=jnp.float32
                )

            def grad_of(turn, scores):
                halves = []
                for h in range(TOGETHER):
                    parts = []
                    for t in range(chunk_tiles):
                        at = slice(turn * chunk_tiles + t, turn * chunk_tiles + t + 1)
                        part = scores[h * BLOCK : (h + 1) * BLOCK, t * QTILE : (t + 1) * QTILE]
                        grown = jnp.exp2(part * log2_scale + bias_now[h, at, :])
                        less = grown - loss_ref[group, at, :]
                        grad = jnp.where(row_ids == rel_now[h, at, :], less, grown)
                        parts.append(grad.astype(jnp.bfloat16))
                    halves.append(jnp.concatenate(parts, axis=1))
                return jnp.concatenate(halves, axis=0)

            def add(turn, logit_grad):
                first = group * group_tiles + turn * chunk_tiles
                added = jnp.dot(logit_grad, load(turn), preferred_element_type=jnp.float32)
                if turn == 0:
                    block_sum[...] = added
                else:
                    block_sum[...] += added
                part = jnp.dot(block_t, logit_grad, preferred_element_type=jnp.float32)
                for t in range(chunk_tiles):
                    dq_ref[first + t] += part[:, t * QTILE : (t + 1) * QTILE]

            scores, before = score(0), None
            for turn in range(turns):
                ahead = score(turn + 1) if turn + 1 < turns else None
                if turn:
                    add(turn - 1, before)
                before = grad_of(turn, scores)
                scores = ahead
            add(turns - 1, before)
            for h in range(TOGETHER):
                total = block_sum[h * BLOCK : (h + 1) * BLOCK, :] * score_scale
                grads[rows[h], :] += total.astype(jnp.bfloat16).astype(jnp.float32)

    store = pltpu.make_async_copy(grads.at[pl.ds(0, row_count), :], index_grad_ref, sems.at[2])
    store.start()
    other_grad_ref[...] = grads[row_count:, :].astype(jnp.bfloat16)
    store.wait()


def work(fetch_all, index_rows, index_other, query_all, small, fetch_count, score_scale):
    row_count, feat_width = index_rows.shape
    groups, group_tiles, _ = small[0].shape
    tile_total = groups * group_tiles
    smem, vmem, anywhere = (
        pl.BlockSpec(memory_space=m) for m in (pltpu.SMEM, pltpu.VMEM, pl.ANY)
    )
    names = (groups, fetch_all.shape[0] // groups * fetch_count + TOGETHER)
    return pl.pallas_call(
        functools.partial(work_kernel, score_scale, groups, fetch_count),
        out_shape=(
            jax.ShapeDtypeStruct((tile_total, feat_width, QTILE), jnp.float32),
            jax.ShapeDtypeStruct(index_rows.shape, jnp.float32),
            jax.ShapeDtypeStruct(index_rows.shape, jnp.bfloat16),
        ),
        in_specs=[smem] + [anywhere] * 2 + [vmem] * 5,
        out_specs=[vmem, anywhere, vmem],
        scratch_shapes=[
            pltpu.SMEM(names, jnp.int32),
            pltpu.SMEM(names, jnp.int32),
            pltpu.VMEM((2 * row_count, feat_width), jnp.bfloat16),
            pltpu.VMEM((2 * row_count, feat_width), jnp.float32),
            pltpu.VMEM((TOGETHER, group_tiles, QTILE), jnp.float32),
            pltpu.VMEM((TOGETHER, group_tiles, QTILE), jnp.int32),
            pltpu.VMEM((TOGETHER * BLOCK, feat_width), jnp.float32),
            pltpu.VMEM((groups, group_tiles, QTILE), jnp.float32),
            pltpu.SemaphoreType.DMA((3,)),
        ],
        compiler_params=pltpu.CompilerParams(vmem_limit_bytes=VMEM_LIMIT),
    )(fetch_all, index_rows, index_other, query_all, *small)


def scatter_kernel(
    y_count,
    z_count,
    x_count,
    score_scale,
    part_ref,
    grad_ref,
    out_ref,
    grad_other,
    plane_send,
    plane_recv,
    column_send,
    column_recv,
    a_sem,
    *sems,
):
    y, core, z, x = coordinates(x_count)
    narrow_count = z_count * x_count
    b_send, b_recv, c_send, c_recv = sems

    def device(dy, dz, dx):
        wide = lax.rem(y + dy, y_count) * CORES + core
        return wide, lax.rem(z + dz, z_count) * x_count + lax.rem(x + dx, x_count)

    def number(place):
        return place[0] // CORES * narrow_count + place[1]

    def remote(source, target, send_sem, recv_sem, peer):
        return pltpu.make_async_remote_copy(
            src_ref=source,
            dst_ref=target,
            send_sem=send_sem,
            recv_sem=recv_sem,
            device_id=peer,
            device_id_type=MESH,
        )

    shifts = [(dy, dx) for dy in range(y_count) for dx in range(x_count)]
    buddy = (y * CORES + 1 - core, z * x_count + x)
    z_peers = [device(0, dz, 0) for dz in range(1, z_count)]
    plane_peers = [device(dy, 0, dx) for dy, dx in shifts[1:]]
    greet(z_peers + plane_peers + [buddy])
    z_order = list(range(1, z_count)) + [0]
    to_buddy = remote(grad_ref, grad_other, a_sem.at[0], a_sem.at[1], buddy)
    to_buddy.start()
    in_plane, columns = {}, {}
    for dz in z_order:
        for p in range(1, len(shifts)):
            slot = (p - 1) * z_count + dz
            dy, dx = shifts[p]
            plane_send[slot] = part_ref[number(device(dy, dz, dx))].astype(jnp.bfloat16)
            in_plane[p, dz] = remote(
                plane_send.at[slot],
                plane_recv.at[slot],
                b_send.at[slot],
                b_recv.at[slot],
                plane_peers[p - 1],
            )
            in_plane[p, dz].start()
    for dz in z_order:
        total = part_ref[number(device(0, dz, 0))]
        for p in range(1, len(shifts)):
            in_plane[p, dz].wait_recv()
            total += plane_recv[(p - 1) * z_count + dz].astype(jnp.float32)
        if dz:
            column_send[dz - 1] = total.astype(jnp.bfloat16)
            columns[dz] = remote(
                column_send.at[dz - 1],
                column_recv.at[dz - 1],
                c_send.at[dz - 1],
                c_recv.at[dz - 1],
                z_peers[dz - 1],
            )
            columns[dz].start()
    for dz in range(1, z_count):
        columns[dz].wait_recv()
        total += column_recv[dz - 1].astype(jnp.float32)
    for t in range(total.shape[0]):
        out_ref[t * QTILE : (t + 1) * QTILE, :] = total[t].T * score_scale
    for copy in [*in_plane.values(), *columns.values()]:
        copy.wait_send()
    to_buddy.wait()


def scatter_all(partial, other_grad, counts, score_scale):
    y_count, z_count, x_count = counts
    devices, tiles, feat_width, width = partial.shape
    passed = devices - z_count
    block = (tiles, feat_width, width)
    vmem, anywhere = (pl.BlockSpec(memory_space=m) for m in (pltpu.VMEM, pl.ANY))
    return pl.pallas_call(
        functools.partial(scatter_kernel, *counts, score_scale),
        out_shape=(
            jax.ShapeDtypeStruct((tiles * width, feat_width), jnp.float32),
            jax.ShapeDtypeStruct(other_grad.shape, other_grad.dtype),
        ),
        in_specs=[vmem, anywhere],
        out_specs=[vmem, anywhere],
        scratch_shapes=[
            pltpu.VMEM((passed, *block), jnp.bfloat16),
            pltpu.VMEM((passed, *block), jnp.bfloat16),
            pltpu.VMEM((z_count - 1, *block), jnp.bfloat16),
            pltpu.VMEM((z_count - 1, *block), jnp.bfloat16),
            pltpu.SemaphoreType.DMA((2,)),
            pltpu.SemaphoreType.DMA((passed,)),
            pltpu.SemaphoreType.DMA((passed,)),
            pltpu.SemaphoreType.DMA((z_count - 1,)),
            pltpu.SemaphoreType.DMA((z_count - 1,)),
        ],
        compiler_params=pltpu.CompilerParams(
            collective_id=1, has_side_effects=True, vmem_limit_bytes=VMEM_LIMIT
        ),
    )(partial, other_grad)


def shards(
    queries, index_rows, lse_shift, loss_weight, positives, tile_negs, fetch_owner, fetch_local
):
    wide_count = lax.axis_size("wide")
    narrow_count = lax.axis_size("narrow")
    devices = wide_count // CORES * narrow_count
    counts = place_counts(wide_count, narrow_count)
    feat_width = queries.shape[1]
    own_queries = queries.shape[0]
    fetch_count = fetch_local.shape[0]
    score_scale = 2.0 / math.sqrt(feat_width)
    named = jnp.concatenate([fetch_owner[:, 0], fetch_local])
    padded = -(-2 * fetch_count // LANES) * LANES
    named = jnp.pad(named, (0, padded - 2 * fetch_count)).reshape(1, padded)
    small = [a.reshape(-1, QTILE) for a in (lse_shift, loss_weight, positives)] + [tile_negs]
    query_all, fetch_all, index_other, *small = gather_all(
        queries, named, index_rows, small, counts
    )
    partial, index_grad, other_grad = work(
        fetch_all,
        index_rows,
        index_other,
        query_all.reshape(-1, feat_width),
        small,
        fetch_count,
        score_scale,
    )
    tiles = own_queries // QTILE
    query_grad, more_grad = scatter_all(
        partial.reshape(devices, tiles, feat_width, QTILE), other_grad, counts, score_scale
    )
    return query_grad, index_grad + more_grad.astype(jnp.float32)


def solution(mesh):
    in_specs = (
        P(("wide", "narrow"), None),
        P(("wide", "narrow"), None),
        P("wide"),
        P("wide"),
        P("wide"),
        P("wide", None),
        P(("wide", "narrow"), None),
        P(("wide", "narrow")),
    )
    out_specs = (P(("wide", "narrow"), None), P(("wide", "narrow"), None))
    return jax.shard_map(shards, mesh=mesh, in_specs=in_specs, out_specs=out_specs, check_vma=False)
```
